1024 devices in a mesh: inner: 64 (over x_hi, z, core), outer: 16 (over x_lo, y).
Axes of the slice: x: 8 (x_hi: 4, x_lo: 2; x = x_hi * 2 + x_lo), y: 8, z: 8, core: 2. Of those that a mesh axis runs over, the one named last changes fastest.
Arguments:
- grads: bfloat16 [16, 64, 1048576], P('outer', 'inner'), may hold values from -1.5 to 1.5, as said below
- master: float32 [1048576], P(('inner', 'outer')), may hold values from -3 to 3
- moment: float32 [1048576], P(('inner', 'outer')), may hold values from -2 to 2
- second: float32 [1048576], P(('inner', 'outer')), may hold values from 0.05 to 2
Outputs:
- params_full: bfloat16 [1048576], P('inner')
- new_master: float32 [1048576], P(('inner', 'outer'))
- new_moment: float32 [1048576], P(('inner', 'outer'))
- new_second: float32 [1048576], P(('inner', 'outer'))
The draws below stay inside these ranges and needn't reach their ends.
Inputs may be any that keep to these rules, and one draw needn't show every extreme that they name: `grads`: gradient values are real-valued, of magnitude at most 48 / sqrt(1024).
All inputs are finite; a program needn't handle non-finite values.
Results may differ from the reference program's by a relative error of at most 0.015.
Values may be sent and summed in bfloat16 or wider, within the bound.
A program may use at most 32 MiB of HBM per device.

```python
import math
import jax
import jax.numpy as jnp
from jax import lax

QB = 2048
SHARE = 1024
STEP = 100
BUCKET = 1048576
N_INNER = 64
N_OUTER = 16


def draw_grads(key, part):
    key = jax.random.fold_in(key, 11)
    key_noise, key_rough = jax.random.split(key, 2)
    devices_all = N_OUTER * N_INNER
    base = 1.0 / math.sqrt(devices_all)
    position = jnp.arange(BUCKET, dtype=jnp.float32) / BUCKET
    ramp = 1.0 + 2.0 * position
    rough = jnp.exp(jax.random.uniform(key_rough, (BUCKET,), jnp.float32, math.log(0.5), math.log(2.0)))
    shape = (N_OUTER, N_INNER, BUCKET)
    noise = jnp.clip(jax.random.normal(key_noise, shape, jnp.float32), -4.0, 4.0)
    values = base * noise * ramp * rough
    return values.astype(jnp.bfloat16)


def steps_of(key, dims, cuts, least, high):
    gain = 1.0
    for dim, blocks in cuts:
        draws = jax.random.uniform(jax.random.fold_in(jax.random.fold_in(key, 6), dim), (blocks,), jnp.float32, least / len(cuts), high / len(cuts))
        gain = gain * jnp.repeat(jnp.exp(draws), dims[dim] // blocks).reshape((-1,) + (1,) * (len(dims) - 1 - dim))
    return gain


def normal_values(stream_key, shape, scale, reach, cuts=(), kind=jnp.bfloat16):
    level = steps_of(stream_key, shape, cuts, -0.22, 0.18) if cuts else 1.0
    drawn = jax.random.normal(stream_key, shape, jnp.float32) * scale * level
    return jnp.minimum(jnp.maximum(drawn, -reach), reach).astype(kind)


def setup_inputs(seed: int = 0) -> dict:
    arg_keys = jax.random.split(jax.random.key(seed), 5)
    grads = draw_grads(jax.random.fold_in(arg_keys[4], 71), 0)
    master = normal_values(arg_keys[1], (BUCKET,), 0.5, 3.0, ((0, 1024),), jnp.float32)
    moment = normal_values(arg_keys[2], (BUCKET,), 0.3, 2.0, ((0, 1024),), jnp.float32)
    second = jnp.clip(jnp.exp(math.log(2.0) - 3.6888794 * jax.random.uniform(arg_keys[3], (BUCKET,), jnp.float32) ** steps_of(arg_keys[3], (BUCKET,), ((0, 1024),), -0.2, 0.2)), 0.05, 2.0)
    return {"grads": grads, "master": master, "moment": moment, "second": second}


beta_one = 0.9
beta_two = 0.95
adam_eps = 1e-08
learn_rate = 0.01
weight_decay = 0.1

def quantize(values):
    largest = lax.optimization_barrier(jnp.max(jnp.abs(values), axis=-1))
    scales = largest + 1e-06
    levels = (values / scales[..., None]).astype(jnp.bfloat16)
    return (levels, scales)

def restore(levels, scales):
    return levels.astype(jnp.float32) * scales[..., None]

def adamw(gradient, master, moment, second):
    new_moment = beta_one * moment + (1.0 - beta_one) * gradient
    new_second = beta_two * second + (1.0 - beta_two) * gradient * gradient
    first_corr = 1.0 - beta_one ** STEP
    second_corr = 1.0 - beta_two ** STEP
    direction = new_moment / first_corr / (jnp.sqrt(new_second / second_corr) + adam_eps)
    new_master = master - learn_rate * (direction + weight_decay * master)
    return (new_master, new_moment, new_second)

def reference(grads, master, moment, second):
    blocks = BUCKET // QB

    def group_sum(local):
        levels, scales = quantize(local.astype(jnp.float32).reshape(N_INNER, blocks, QB))
        partial_value = lax.optimization_barrier(jnp.sum(restore(levels, scales), axis=0)).reshape(BUCKET // SHARE, SHARE)
        levels_two, scales_two = quantize(partial_value)
        return restore(levels_two, scales_two).reshape(BUCKET)
    restored = lax.map(group_sum, grads)
    gradient = lax.optimization_barrier(jnp.sum(restored, axis=0))
    new_master, new_moment, new_second = adamw(gradient, master, moment, second)
    params_full = new_master.astype(jnp.bfloat16)
    return (params_full, new_master, new_moment, new_second)
```

```python
import jax
import jax.numpy as jnp
from jax import lax
from jax.experimental import pallas as pl
from jax.experimental.pallas import tpu as pltpu
from jax.sharding import PartitionSpec as P

STEP = 100

beta_one = 0.9
beta_two = 0.95
adam_eps = 1e-08
learn_rate = 0.01
weight_decay = 0.1

MESH = pl.DeviceIdType.MESH
RING = 8
SHARE = 1024
ORDER = (4, 3, 5, 2, 6, 1, 7)


def adamw(gradient, master, moment, second):
    new_moment = beta_one * moment + (1.0 - beta_one) * gradient
    new_second = beta_two * second + (1.0 - beta_two) * gradient * gradient
    first_corr = 1.0 - beta_one**STEP
    second_corr = 1.0 - beta_two**STEP
    direction = new_moment / first_corr / (jnp.sqrt(new_second / second_corr) + adam_eps)
    new_master = master - learn_rate * (direction + weight_decay * master)
    return (new_master, new_moment, new_second)


def kernel(
    grads, master, moment, second,
    params_out, master_out, moment_out, second_out,
    raw, halves, from_core, from_one, part_one, to_two, from_two, part_two, from_three, state, fresh,
    load_sem, state_sem, core_send, core_recv, one_send, one_recv, two_send, two_recv,
    three_send, three_recv, all_send, all_recv,
):
    inner, outer = lax.axis_index("inner"), lax.axis_index("outer")
    x_hi, z, core = inner // 16, (inner // 2) % 8, inner % 2
    x_lo, y = outer // 8, outer % 8
    x = x_hi * 2 + x_lo

    def place(x, y, z, core):
        return ((x // 2) * 16 + z * 2 + core, (x % 2) * 8 + y)

    def along(axis, step):
        cx = lax.rem(x + step, RING) if axis == "x" else x
        cy = lax.rem(y + step, RING) if axis == "y" else y
        cz = lax.rem(z + step, RING) if axis == "z" else z
        return place(cx, cy, cz, core)

    first = jnp.where(core == 0, z, x)
    mate_first = jnp.where(core == 0, x, z)
    second_at = jnp.where(core == 0, y, z)
    third = jnp.where(core == 0, x, y)

    def peer(stage, step):
        on_zero = along(("z", "y", "x")[stage], step)
        on_one = along(("x", "z", "y")[stage], step)
        return tuple(jnp.where(core == 0, a, b) for a, b in zip(on_zero, on_one))

    mate = (inner + 1 - 2 * core, outer)

    parts = 8
    size = grads.shape[-1] // parts
    loads = [
        pltpu.make_async_copy(
            grads.at[:, :, pl.ds(i * size, size)], raw.at[:, :, pl.ds(i * size, size)], load_sem.at[i]
        )
        for i in range(parts)
    ]
    for load in loads:
        load.start()
    state_loads = [
        pltpu.make_async_copy(ref, state.at[i], state_sem.at[i])
        for i, ref in enumerate((master, moment, second))
    ]
    for load in state_loads:
        load.start()

    barrier = pltpu.get_barrier_semaphore()
    count = 0
    for step in ORDER:
        for axis in ("x", "y", "z"):
            pl.semaphore_signal(barrier, inc=1, device_id=along(axis, step), device_id_type=MESH)
            count += 1
    for step in range(1, RING):
        other = (inner, (1 - x_lo) * 8 + lax.rem(y + step, RING))
        pl.semaphore_signal(barrier, inc=1, device_id=other, device_id_type=MESH)
        count += 1
    pl.semaphore_signal(barrier, inc=1, device_id=mate, device_id_type=MESH)
    count += 1

    per_load = 4
    block = SHARE * 16
    for i in range(parts):
        loads[i].wait()

        def pack(j, carry):
            at_hi, at_z = i // 2, (i % 2) * 4 + j
            base = pl.multiple_of(i * size + j * 2 * block, block)
            zero = raw[0, :, pl.ds(base, block)].astype(jnp.float32).reshape(2, 8, 8, 128)
            pair = jnp.concatenate([zero[0], zero[1]], axis=1)
            halves[0, at_z, :, at_hi] = pair.astype(jnp.bfloat16)
            one = raw[0, :, pl.ds(pl.multiple_of(base + block, block), block)]
            one = one.astype(jnp.float32).reshape(2, 4, 16, 128).astype(jnp.bfloat16)
            halves[1, at_hi * 2, at_z] = one[0]
            halves[1, at_hi * 2 + 1, at_z] = one[1]
            return carry

        lax.fori_loop(0, per_load, pack, 0)

    pl.semaphore_wait(barrier, count)

    steps = ORDER + (0,)
    core_copies = []
    for k, step in enumerate(steps):
        copy = pltpu.make_async_remote_copy(
            src_ref=halves.at[1 - core, lax.rem(mate_first + step, RING)],
            dst_ref=from_core.at[k],
            send_sem=core_send.at[k],
            recv_sem=core_recv.at[k],
            device_id=mate,
            device_id_type=MESH,
        )
        copy.start()
        core_copies.append(copy)

    one_copies = []
    for k, step in enumerate(steps):
        core_copies[k].wait_recv()
        at = lax.rem(first + step, RING)
        if step:
            for t in range(8):
                total = halves[core, at, t].astype(jnp.float32) + from_core[k, t].astype(jnp.float32)
                halves[core, at, t] = total.astype(jnp.bfloat16)
            copy = pltpu.make_async_remote_copy(
                src_ref=halves.at[core, at],
                dst_ref=from_one.at[k],
                send_sem=one_send.at[k],
                recv_sem=one_recv.at[k],
                device_id=peer(0, step),
                device_id_type=MESH,
            )
            copy.start()
            one_copies.append(copy)
        else:
            for t in range(8):
                part_one[t] = halves[core, at, t].astype(jnp.float32) + from_core[k, t].astype(jnp.float32)
    for k, step in enumerate(ORDER):
        one_copies[k].wait_recv()
        for t in range(8):
            part_one[t] += from_one[k, t].astype(jnp.float32)

    two_copies = []
    for k, step in enumerate(ORDER):
        to_two[k] = part_one[lax.rem(second_at + step, RING)].astype(jnp.bfloat16)
        copy = pltpu.make_async_remote_copy(
            src_ref=to_two.at[k],
            dst_ref=from_two.at[k],
            send_sem=two_send.at[k],
            recv_sem=two_recv.at[k],
            device_id=peer(1, step),
            device_id_type=MESH,
        )
        copy.start()
        two_copies.append(copy)
    total = part_one[second_at]
    for copy in two_copies[::-1]:
        copy.wait_recv()
    for k in range(len(ORDER)):
        total += from_two[k].astype(jnp.float32)
    part_two[...] = total.reshape(8, 8, 128)

    three_copies = []
    for k, step in enumerate(ORDER):
        copy = pltpu.make_async_remote_copy(
            src_ref=part_two.at[lax.rem(third + step, RING)],
            dst_ref=from_three.at[k],
            send_sem=three_send.at[k],
            recv_sem=three_recv.at[k],
            device_id=peer(2, step),
            device_id_type=MESH,
        )
        copy.start()
        three_copies.append(copy)
    for load in state_loads:
        load.wait()
    gradient = part_two[third]
    for copy in three_copies[::-1]:
        copy.wait_recv()
    for k in range(len(ORDER)):
        gradient += from_three[k]

    new_master, new_moment, new_second = adamw(gradient, state[0], state[1], state[2])
    fresh[outer] = new_master

    all_copies = []
    for step in ORDER + (0,):
        for flip in (1, 0):
            if step or flip:
                k = len(all_copies)
                other = (x_lo + flip - 2 * flip * x_lo) * 8 + lax.rem(y + step, RING)
                copy = pltpu.make_async_remote_copy(
                    src_ref=fresh.at[outer],
                    dst_ref=fresh.at[outer],
                    send_sem=all_send.at[k],
                    recv_sem=all_recv.at[k],
                    device_id=(inner, other),
                    device_id_type=MESH,
                )
                copy.start()
                all_copies.append(copy)
    master_out[...] = new_master
    moment_out[...] = new_moment
    second_out[...] = new_second
    for copies in (core_copies, one_copies, two_copies, three_copies):
        for copy in copies:
            copy.wait_send()
    for copy in all_copies[::-1]:
        copy.wait_recv()
    params_out[...] = fresh[...].reshape(128, 128).astype(jnp.bfloat16)
    for copy in all_copies:
        copy.wait_send()


def per_device(grads, master, moment, second):
    shares = [a.reshape(8, 128) for a in (master, moment, second)]
    bf16, f32 = jnp.bfloat16, jnp.float32
    vmem = pl.BlockSpec(memory_space=pltpu.VMEM)
    hbm = pl.BlockSpec(memory_space=pl.ANY)
    dma = pltpu.SemaphoreType.DMA
    others = len(ORDER)
    params, *outs = pl.pallas_call(
        kernel,
        out_shape=[jax.ShapeDtypeStruct((128, 128), bf16)] + [jax.ShapeDtypeStruct((8, 128), f32)] * 3,
        in_specs=[hbm] * 4,
        out_specs=[vmem] * 4,
        scratch_shapes=[
            pltpu.VMEM(grads.shape, bf16),
            pltpu.VMEM((2, 8, 8, 4, 16, 128), bf16),
            pltpu.VMEM((8, 8, 4, 16, 128), bf16),
            pltpu.VMEM((others, 8, 4, 16, 128), bf16),
            pltpu.VMEM((8, 4, 16, 128), f32),
            pltpu.VMEM((others, 4, 16, 128), bf16),
            pltpu.VMEM((others, 4, 16, 128), bf16),
            pltpu.VMEM((8, 8, 128), f32),
            pltpu.VMEM((others, 8, 128), f32),
            pltpu.VMEM((3, 8, 128), f32),
            pltpu.VMEM((16, 8, 128), f32),
            dma((8,)), dma((3,)),
            dma((8,)), dma((8,)),
            dma((others,)), dma((others,)),
            dma((others,)), dma((others,)),
            dma((others,)), dma((others,)),
            dma((15,)), dma((15,)),
        ],
        compiler_params=pltpu.CompilerParams(
            collective_id=0, has_side_effects=True, vmem_limit_bytes=48 << 20
        ),
    )(grads, *shares)
    return (params.reshape(-1), *(a.reshape(-1) for a in outs))


def solution(mesh):
    in_specs = (
        P("outer", "inner", None),
        P(("inner", "outer")),
        P(("inner", "outer")),
        P(("inner", "outer")),
    )
    out_specs = (P("inner"), P(("inner", "outer")), P(("inner", "outer")), P(("inner", "outer")))
    return jax.shard_map(
        per_device, mesh=mesh, in_specs=in_specs, out_specs=out_specs, check_vma=False
    )
```

```python
import jax
import jax.numpy as jnp
from jax import lax
from jax.experimental import pallas as pl
from jax.experimental.pallas import tpu as pltpu
from jax.sharding import PartitionSpec as P

STEP = 100

beta_one = 0.9
beta_two = 0.95
adam_eps = 1e-08
learn_rate = 0.01
weight_decay = 0.1

MESH = pl.DeviceIdType.MESH
VMEM_LIMIT = 60 << 20
RING = 8
SHARE = 1024
ORDER = (4, 3, 5, 2, 6, 1, 7)


def adamw(gradient, master, moment, second):
    new_moment = beta_one * moment + (1.0 - beta_one) * gradient
    new_second = beta_two * second + (1.0 - beta_two) * gradient * gradient
    first_corr = 1.0 - beta_one**STEP
    second_corr = 1.0 - beta_two**STEP
    direction = new_moment / first_corr / (jnp.sqrt(new_second / second_corr) + adam_eps)
    new_master = master - learn_rate * (direction + weight_decay * master)
    return (new_master, new_moment, new_second)


CUT = 5


def kernel(
    grads, master, moment, second, result,
    raw, half_a, half_b, core_a, core_b, from_a, from_b, part_one, to_two, from_two, part_two,
    from_three, state,
    load_sem, state_sem, core_send, core_recv, one_send, one_recv, two_send, two_recv,
    three_send, three_recv, all_send, all_recv,
):
    inner, outer = lax.axis_index("inner"), lax.axis_index("outer")
    x_hi, z, core = inner // 16, (inner // 2) % 8, inner % 2
    x_lo, y = outer // 8, outer % 8
    x = x_hi * 2 + x_lo

    def place(x, y, z):
        return ((x // 2) * 16 + z * 2 + core, (x % 2) * 8 + y)

    def along(axis, step):
        cx = lax.rem(x + step, RING) if axis == "x" else x
        cy = lax.rem(y + step, RING) if axis == "y" else y
        cz = lax.rem(z + step, RING) if axis == "z" else z
        return place(cx, cy, cz)

    def pick(condition, a, b):
        return tuple(jnp.where(condition, p, q) for p, q in zip(a, b))

    zero = core == 0
    near = jnp.where(zero, z, y)
    mate_near = jnp.where(zero, y, z)
    slab = jnp.where(zero, y, z)
    low = slab < CUT
    third = jnp.where(low, x, jnp.where(zero, z, y))

    def peer_a(step):
        return pick(zero, along("z", step), along("y", step))

    def peer_b(step):
        return along("x", step)

    def peer_two(step):
        return pick(zero, along("y", step), along("z", step))

    def peer_three(step):
        return pick(low, along("x", step), pick(zero, along("z", step), along("y", step)))

    mate = (inner + 1 - 2 * core, outer)

    parts = 8
    size = grads.shape[-1] // parts
    loads = [
        pltpu.make_async_copy(
            grads.at[:, :, pl.ds(i * size, size)], raw.at[:, :, pl.ds(i * size, size)], load_sem.at[i]
        )
        for i in range(parts)
    ]
    for load in loads:
        load.start()
    state_loads = [
        pltpu.make_async_copy(ref, state.at[i], state_sem.at[i])
        for i, ref in enumerate((master, moment, second))
    ]
    for load in state_loads:
        load.start()

    barrier = pltpu.get_barrier_semaphore()
    count = 0
    for step in ORDER:
        for axis in ("x", "y", "z"):
            pl.semaphore_signal(barrier, inc=1, device_id=along(axis, step), device_id_type=MESH)
            count += 1
    for step in range(1, RING):
        other = (inner, (1 - x_lo) * 8 + lax.rem(y + step, RING))
        pl.semaphore_signal(barrier, inc=1, device_id=other, device_id_type=MESH)
        count += 1
    pl.semaphore_signal(barrier, inc=1, device_id=mate, device_id_type=MESH)
    count += 1

    block = SHARE * 16

    def piece(at_hi, at_z, at_core):
        base = pl.multiple_of(((at_hi * 8 + at_z) * 2 + at_core) * block, block)
        return raw[0, :, pl.ds(base, block)].astype(jnp.float32).reshape(2, 8, 8, 128)

    def tile(a, b):
        return jnp.concatenate([a, b], axis=-2).astype(jnp.bfloat16)

    for part in range(parts):
        loads[part].wait()
        at_hi = part // 2
        for at_z in range(part % 2 * 4, part % 2 * 4 + 4, 2):
            even, odd = piece(at_hi, at_z, 0), piece(at_hi, at_z + 1, 0)
            half_a[0, at_z, :, at_hi] = tile(even[0, :CUT], even[1, :CUT])
            half_a[0, at_z + 1, :, at_hi] = tile(odd[0, :CUT], odd[1, :CUT])
            for lo in range(2):
                half_b[0, at_hi * 2 + lo, :, at_z // 2] = tile(even[lo, CUT:], odd[lo, CUT:])
            for slab_z in (at_z, at_z + 1):
                values = piece(at_hi, slab_z, 1)
                if slab_z < CUT:
                    half_a[1, :, slab_z, at_hi] = tile(values[0], values[1])
                else:
                    for lo in range(2):
                        half_b[1, at_hi * 2 + lo, slab_z - CUT] = values[lo].reshape(4, 16, 128).astype(jnp.bfloat16)

    pl.semaphore_wait(barrier, count)

    def send(src, dst, send_sem, recv_sem, to):
        copy = pltpu.make_async_remote_copy(
            src_ref=src, dst_ref=dst, send_sem=send_sem, recv_sem=recv_sem, device_id=to, device_id_type=MESH
        )
        copy.start()
        return copy

    steps = ORDER + (0,)
    core_copies = []
    for k, step in enumerate(steps):
        for p, half, arrived, at in ((0, half_a, core_a, mate_near), (1, half_b, core_b, x)):
            core_copies.append(send(
                half.at[1 - core, lax.rem(at + step, RING)], arrived.at[k],
                core_send.at[p, k], core_recv.at[p, k], mate,
            ))

    one_copies = []
    for k, step in enumerate(steps):
        for p, half, arrived, landed, at, peer in (
            (0, half_a, core_a, from_a, near, peer_a),
            (1, half_b, core_b, from_b, x, peer_b),
        ):
            core_copies[2 * k + p].wait_recv()
            at = lax.rem(at + step, RING)
            for t in range(arrived.shape[1]):
                total = half[core, at, t].astype(jnp.float32) + arrived[k, t].astype(jnp.float32)
                if step:
                    half[core, at, t] = total.astype(jnp.bfloat16)
                else:
                    part_one[p * CUT + t] = total
            if step:
                one_copies.append(send(
                    half.at[core, at], landed.at[k], one_send.at[p, k], one_recv.at[p, k], peer(step)
                ))
    for k, step in enumerate(ORDER):
        for p, landed in enumerate((from_a, from_b)):
            one_copies[2 * k + p].wait_recv()
            for t in range(landed.shape[1]):
                part_one[p * CUT + t] += landed[k, t].astype(jnp.float32)

    two_copies = []
    for k, step in enumerate(ORDER):
        to_two[k] = part_one[lax.rem(slab + step, RING)].astype(jnp.bfloat16)
        two_copies.append(send(to_two.at[k], from_two.at[k], two_send.at[k], two_recv.at[k], peer_two(step)))
    total = part_one[slab]
    for copy in two_copies[::-1]:
        copy.wait_recv()
    for k in range(len(ORDER)):
        total += from_two[k].astype(jnp.float32)
    part_two[...] = total.reshape(8, 8, 128)

    three_copies = []
    for k, step in enumerate(ORDER):
        three_copies.append(send(
            part_two.at[lax.rem(third + step, RING)], from_three.at[k],
            three_send.at[k], three_recv.at[k], peer_three(step),
        ))
    for load in state_loads:
        load.wait()
    gradient = part_two[third]
    for copy in three_copies[::-1]:
        copy.wait_recv()
    for k in range(len(ORDER)):
        gradient += from_three[k]

    new_master, new_moment, new_second = adamw(gradient, state[0], state[1], state[2])
    result[outer] = new_master

    all_copies = []
    for step in ORDER + (0,):
        for flip in (1, 0):
            if step or flip:
                k = len(all_copies)
                other = (x_lo + flip - 2 * flip * x_lo) * 8 + lax.rem(y + step, RING)
                all_copies.append(send(
                    result.at[outer], result.at[outer], all_send.at[k], all_recv.at[k], (inner, other)
                ))
    result[16] = new_master
    result[17] = new_moment
    result[18] = new_second
    for copies in (core_copies, one_copies, two_copies, three_copies):
        for copy in copies:
            copy.wait_send()
    for copy in all_copies[::-1]:
        copy.wait_recv()
    for copy in all_copies:
        copy.wait_send()


def finish(result, params_out, master_out, moment_out, second_out):
    params_out[...] = result[:16].reshape(128, 128).astype(jnp.bfloat16)
    master_out[...] = result[16]
    moment_out[...] = result[17]
    second_out[...] = result[18]


def per_device(grads, master, moment, second):
    shares = [a.reshape(8, 128) for a in (master, moment, second)]
    bf16, f32 = jnp.bfloat16, jnp.float32
    vmem = pl.BlockSpec(memory_space=pltpu.VMEM)
    hbm = pl.BlockSpec(memory_space=pl.ANY)
    dma = pltpu.SemaphoreType.DMA
    others = len(ORDER)
    rest = RING - CUT
    result = pl.pallas_call(
        kernel,
        out_shape=jax.ShapeDtypeStruct((19, 8, 128), f32),
        in_specs=[hbm] * 4,
        out_specs=vmem,
        scratch_shapes=[
            pltpu.VMEM(grads.shape, bf16),
            pltpu.VMEM((2, 8, CUT, 4, 16, 128), bf16),
            pltpu.VMEM((2, 8, rest, 4, 16, 128), bf16),
            pltpu.VMEM((8, CUT, 4, 16, 128), bf16),
            pltpu.VMEM((8, rest, 4, 16, 128), bf16),
            pltpu.VMEM((others, CUT, 4, 16, 128), bf16),
            pltpu.VMEM((others, rest, 4, 16, 128), bf16),
            pltpu.VMEM((8, 4, 16, 128), f32),
            pltpu.VMEM((others, 4, 16, 128), bf16),
            pltpu.VMEM((others, 4, 16, 128), bf16),
            pltpu.VMEM((8, 8, 128), f32),
            pltpu.VMEM((others, 8, 128), f32),
            pltpu.VMEM((3, 8, 128), f32),
            dma((8,)), dma((3,)),
            dma((2, 8)), dma((2, 8)),
            dma((2, others)), dma((2, others)),
            dma((others,)), dma((others,)),
            dma((others,)), dma((others,)),
            dma((15,)), dma((15,)),
        ],
        compiler_params=pltpu.CompilerParams(
            collective_id=0, has_side_effects=True, vmem_limit_bytes=VMEM_LIMIT
        ),
    )(grads, *shares)
    params, *outs = pl.pallas_call(
        finish,
        out_shape=[jax.ShapeDtypeStruct((128, 128), bf16)] + [jax.ShapeDtypeStruct((8, 128), f32)] * 3,
        in_specs=[vmem],
        out_specs=[vmem] * 4,
        compiler_params=pltpu.CompilerParams(vmem_limit_bytes=VMEM_LIMIT),
    )(result)
    return (params.reshape(-1), *(a.reshape(-1) for a in outs))


def solution(mesh):
    in_specs = (
        P("outer", "inner", None),
        P(("inner", "outer")),
        P(("inner", "outer")),
        P(("inner", "outer")),
    )
    out_specs = (P("inner"), P(("inner", "outer")), P(("inner", "outer")), P(("inner", "outer")))
    return jax.shard_map(
        per_device, mesh=mesh, in_specs=in_specs, out_specs=out_specs, check_vma=False
    )
```

```python
import jax
import jax.numpy as jnp
from jax import lax
from jax.experimental import pallas as pl
from jax.experimental.pallas import tpu as pltpu
from jax.sharding import PartitionSpec as P

STEP = 100

beta_one = 0.9
beta_two = 0.95
adam_eps = 1e-08
learn_rate = 0.01
weight_decay = 0.1

MESH = pl.DeviceIdType.MESH
VMEM_LIMIT = 32 << 20
RING = 8
SHARE = 1024
ORDER = (4, 3, 5, 2, 6, 1, 7)


def adamw(gradient, master, moment, second):
    new_moment = beta_one * moment + (1.0 - beta_one) * gradient
    new_second = beta_two * second + (1.0 - beta_two) * gradient * gradient
    first_corr = 1.0 - beta_one**STEP
    second_corr = 1.0 - beta_two**STEP
    direction = new_moment / first_corr / (jnp.sqrt(new_second / second_corr) + adam_eps)
    new_master = master - learn_rate * (direction + weight_decay * master)
    return (new_master, new_moment, new_second)


CUT = 5


def kernel(
    grads, master, moment, second, result,
    raw, half_a, half_b, core_a, core_b, from_a, from_b, part_one, from_two, state,
    load_sem, state_sem, core_send, core_recv, one_send, one_recv, two_send, two_recv,
    all_send, all_recv, entered,
):
    inner, outer = lax.axis_index("inner"), lax.axis_index("outer")
    x_hi, z, core = inner // 16, (inner // 2) % 8, inner % 2
    x_lo, y = outer // 8, outer % 8
    x = x_hi * 2 + x_lo

    def place(x, y, z):
        return ((x // 2) * 16 + z * 2 + core, (x % 2) * 8 + y)

    def along(axis, step):
        cx = lax.rem(x + step, RING) if axis == "x" else x
        cy = lax.rem(y + step, RING) if axis == "y" else y
        cz = lax.rem(z + step, RING) if axis == "z" else z
        return place(cx, cy, cz)

    def pick(condition, a, b):
        return tuple(jnp.where(condition, p, q) for p, q in zip(a, b))

    zero = core == 0
    near = jnp.where(zero, z, y)
    mate_near = jnp.where(zero, y, z)
    slab = jnp.where(zero, y, z)
    low = slab < CUT
    side = jnp.where(zero, z, y)

    def peer_a(step):
        return pick(zero, along("z", step), along("y", step))

    def peer_b(step):
        return along("x", step)

    mate = (inner + 1 - 2 * core, outer)

    parts = 8
    size = grads.shape[-1] // parts
    loads = [
        pltpu.make_async_copy(
            grads.at[:, :, pl.ds(i * size, size)], raw.at[:, :, pl.ds(i * size, size)], load_sem.at[i]
        )
        for i in range(parts)
    ]
    for load in loads:
        load.start()
    state_loads = [
        pltpu.make_async_copy(ref, state.at[i], state_sem.at[i])
        for i, ref in enumerate((master, moment, second))
    ]
    for load in state_loads:
        load.start()

    barrier = pltpu.get_barrier_semaphore()

    @pl.when(zero)
    def _():
        pl.semaphore_signal(barrier, inc=1, device_id=mate, device_id_type=MESH)

    count = 0
    for step in ORDER:
        for axis in ("x", "y", "z"):
            to_inner, to_outer = along(axis, step)
            pl.semaphore_signal(barrier, inc=1, device_id=(to_inner - core, to_outer), device_id_type=MESH)
            count += 2

    @pl.when(core == 1)
    def _():
        pl.semaphore_wait(barrier, 1)
        pl.semaphore_signal(entered, inc=1, device_id=mate, device_id_type=MESH)

    block = SHARE * 16

    def piece(at_hi, at_z, at_core):
        base = pl.multiple_of(((at_hi * 8 + at_z) * 2 + at_core) * block, block)
        return raw[0, :, pl.ds(base, block)].astype(jnp.float32).reshape(2, 8, 8, 128)

    def tile(a, b):
        return jnp.concatenate([a, b], axis=-2).astype(jnp.bfloat16)

    for part in range(parts):
        loads[part].wait()
        at_hi = part // 2
        for at_z in range(part % 2 * 4, part % 2 * 4 + 4, 2):
            even, odd = piece(at_hi, at_z, 0), piece(at_hi, at_z + 1, 0)
            half_a[0, at_z, :, at_hi] = tile(even[0, :CUT], even[1, :CUT])
            half_a[0, at_z + 1, :, at_hi] = tile(odd[0, :CUT], odd[1, :CUT])
            for lo in range(2):
                half_b[0, at_hi * 2 + lo, :, at_z // 2] = tile(even[lo, CUT:], odd[lo, CUT:])
            for slab_z in (at_z, at_z + 1):
                values = piece(at_hi, slab_z, 1)
                if slab_z < CUT:
                    half_a[1, :, slab_z, at_hi] = tile(values[0], values[1])
                else:
                    for lo in range(2):
                        half_b[1, at_hi * 2 + lo, slab_z - CUT] = values[lo].reshape(4, 16, 128).astype(jnp.bfloat16)

    @pl.when(zero)
    def _():
        pl.semaphore_wait(entered, 1)

    def send(src, dst, send_sem, recv_sem, to):
        copy = pltpu.make_async_remote_copy(
            src_ref=src, dst_ref=dst, send_sem=send_sem, recv_sem=recv_sem, device_id=to, device_id_type=MESH
        )
        copy.start()
        return copy

    steps = ORDER + (0,)
    core_copies = []
    for k, step in enumerate(steps):
        for p, half, arrived, at in ((0, half_a, core_a, mate_near), (1, half_b, core_b, x)):
            core_copies.append(send(
                half.at[1 - core, lax.rem(at + step, RING)], arrived.at[k],
                core_send.at[p, k], core_recv.at[p, k], mate,
            ))

    @pl.when(zero)
    def _():
        pl.semaphore_wait(barrier, count)
        pl.semaphore_signal(entered, inc=1, device_id=mate, device_id_type=MESH)

    @pl.when(core == 1)
    def _():
        pl.semaphore_wait(entered, 1)

    one_copies = []
    for k, step in enumerate(steps):
        for p, half, arrived, landed, at, peer in (
            (0, half_a, core_a, from_a, near, peer_a),
            (1, half_b, core_b, from_b, x, peer_b),
        ):
            core_copies[2 * k + p].wait_recv()
            at = lax.rem(at + step, RING)
            for t in range(arrived.shape[1]):
                total = half[core, at, t].astype(jnp.float32) + arrived[k, t].astype(jnp.float32)
                if step:
                    half[core, at, t] = total.astype(jnp.bfloat16)
                else:
                    part_one[p * CUT + t] = total.reshape(8, 8, 128)
            if step:
                one_copies.append(send(
                    half.at[core, at], landed.at[k], one_send.at[p, k], one_recv.at[p, k], peer(step)
                ))
    targets = []
    lines = []
    for step in range(RING):
        at_x, at_side = lax.rem(x + step, RING), lax.rem(side + step, RING)
        lines.append((
            at_x, (at_x // 2) * 16, (at_x % 2) * 8,
            at_side, jnp.where(zero, at_side * 2, 0), jnp.where(zero, 0, at_side),
        ))
    for far in range(RING):
        s = lax.rem(slab + far, RING)
        s_low = s < CUT
        low_in, low_out = jnp.where(zero, z * 2, s * 2 + 1), jnp.where(zero, s, y)
        high_in = x_hi * 16 + jnp.where(zero, 0, s * 2 + 1)
        high_out = x_lo * 8 + jnp.where(zero, s, 0)
        slot = slab * 8 + jnp.where(s_low, x, side)
        for step in range(RING):
            if far or step:
                at_x, x_in, x_out, at_side, side_in, side_out = lines[step]
                hops = min(far, RING - far) + min(step, RING - step)
                targets.append((
                    hops, s, jnp.where(s_low, at_x, at_side), slot,
                    jnp.where(s_low, x_in + low_in, side_in + high_in),
                    jnp.where(s_low, x_out + low_out, side_out + high_out),
                ))
    targets.sort(key=lambda target: -target[0])

    for k, step in enumerate(ORDER):
        for p, landed in enumerate((from_a, from_b)):
            one_copies[2 * k + p].wait_recv()
            for t in range(landed.shape[1]):
                part_one[p * CUT + t] += landed[k, t].astype(jnp.float32).reshape(8, 8, 128)

    for _, at_slab, at, slot, to_inner, to_outer in targets:
        send(part_one.at[at_slab, at], from_two.at[slot], two_send, two_recv, (to_inner, to_outer))
    third = jnp.where(low, x, side)
    from_two[slab * 8 + third] = part_one[slab, third]
    for load in state_loads:
        load.wait()
    arrived = from_two.at[pl.ds(0, RING * RING - 1)]
    pltpu.make_async_copy(arrived, arrived, two_recv).wait()
    gradient = jnp.sum(from_two[...], axis=0)

    new_master, new_moment, new_second = adamw(gradient, state[0], state[1], state[2])
    result[outer] = new_master

    all_copies = []
    for step in ORDER + (0,):
        for flip in (1, 0):
            if step or flip:
                k = len(all_copies)
                other = (x_lo + flip - 2 * flip * x_lo) * 8 + lax.rem(y + step, RING)
                all_copies.append(send(
                    result.at[outer], result.at[outer], all_send.at[k], all_recv.at[k], (inner, other)
                ))
    result[16] = new_master
    result[17] = new_moment
    result[18] = new_second
    for copies in (core_copies, one_copies):
        for copy in copies:
            copy.wait_send()
    pltpu.make_async_copy(arrived, arrived, two_send).wait()
    for copy in all_copies[::-1]:
        copy.wait_recv()
    for copy in all_copies:
        copy.wait_send()


def finish(result, params_out, master_out, moment_out, second_out):
    params_out[...] = result[:16].reshape(128, 128).astype(jnp.bfloat16)
    master_out[...] = result[16]
    moment_out[...] = result[17]
    second_out[...] = result[18]


def per_device(grads, master, moment, second):
    shares = [a.reshape(8, 128) for a in (master, moment, second)]
    bf16, f32 = jnp.bfloat16, jnp.float32
    vmem = pl.BlockSpec(memory_space=pltpu.VMEM)
    hbm = pl.BlockSpec(memory_space=pl.ANY)
    dma = pltpu.SemaphoreType.DMA
    others = len(ORDER)
    rest = RING - CUT
    result = pl.pallas_call(
        kernel,
        out_shape=jax.ShapeDtypeStruct((19, 8, 128), f32),
        in_specs=[hbm] * 4,
        out_specs=vmem,
        scratch_shapes=[
            pltpu.VMEM(grads.shape, bf16),
            pltpu.VMEM((2, 8, CUT, 4, 16, 128), bf16),
            pltpu.VMEM((2, 8, rest, 4, 16, 128), bf16),
            pltpu.VMEM((8, CUT, 4, 16, 128), bf16),
            pltpu.VMEM((8, rest, 4, 16, 128), bf16),
            pltpu.VMEM((others, CUT, 4, 16, 128), bf16),
            pltpu.VMEM((others, rest, 4, 16, 128), bf16),
            pltpu.VMEM((8, 8, 8, 128), f32),
            pltpu.VMEM((64, 8, 128), f32),
            pltpu.VMEM((3, 8, 128), f32),
            dma((8,)), dma((3,)),
            dma((2, 8)), dma((2, 8)),
            dma((2, others)), dma((2, others)),
            dma, dma,
            dma((15,)), dma((15,)),
            pltpu.SemaphoreType.REGULAR,
        ],
        compiler_params=pltpu.CompilerParams(
            collective_id=0, has_side_effects=True, vmem_limit_bytes=VMEM_LIMIT
        ),
    )(*(pltpu.with_memory_space_constraint(a, pltpu.HBM) for a in (grads, *shares)))
    params, *outs = pl.pallas_call(
        finish,
        out_shape=[jax.ShapeDtypeStruct((128, 128), bf16)] + [jax.ShapeDtypeStruct((8, 128), f32)] * 3,
        in_specs=[vmem],
        out_specs=[vmem] * 4,
        compiler_params=pltpu.CompilerParams(vmem_limit_bytes=VMEM_LIMIT),
    )(result)
    return (params.reshape(-1), *(a.reshape(-1) for a in outs))


def solution(mesh):
    in_specs = (
        P("outer", "inner", None),
        P(("inner", "outer")),
        P(("inner", "outer")),
        P(("inner", "outer")),
    )
    out_specs = (P("inner"), P(("inner", "outer")), P(("inner", "outer")), P(("inner", "outer")))
    return jax.shard_map(
        per_device, mesh=mesh, in_specs=in_specs, out_specs=out_specs, check_vma=False
    )
```

```python
import jax
import jax.numpy as jnp
from jax import lax
from jax.experimental import pallas as pl
from jax.experimental.pallas import tpu as pltpu
from jax.sharding import PartitionSpec as P

STEP = 100

beta_one = 0.9
beta_two = 0.95
adam_eps = 1e-08
learn_rate = 0.01
weight_decay = 0.1

MESH = pl.DeviceIdType.MESH
VMEM_LIMIT = 32 << 20
RING = 8
SHARE = 1024
ORDER = (4, 3, 5, 2, 6, 1, 7)


def adamw(gradient, master, moment, second):
    new_moment = beta_one * moment + (1.0 - beta_one) * gradient
    new_second = beta_two * second + (1.0 - beta_two) * gradient * gradient
    first_corr = 1.0 - beta_one**STEP
    second_corr = 1.0 - beta_two**STEP
    direction = new_moment / first_corr / (jnp.sqrt(new_second / second_corr) + adam_eps)
    new_master = master - learn_rate * (direction + weight_decay * master)
    return (new_master, new_moment, new_second)


EARLY = 2
CUT = 5


def kernel(
    grads, master, moment, second, result,
    raw, half_a, half_b, core_a, core_b, from_a, from_b, part_one, from_two, state,
    load_sem, state_sem, core_send, core_recv, one_send, one_recv, two_send, two_recv,
    all_send, all_recv, entered, known,
):
    inner, outer = lax.axis_index("inner"), lax.axis_index("outer")
    x_hi, z, core = inner // 16, (inner // 2) % 8, inner % 2
    x_lo, y = outer // 8, outer % 8
    x = x_hi * 2 + x_lo

    def place(x, y, z):
        return ((x // 2) * 16 + z * 2 + core, (x % 2) * 8 + y)

    def along(axis, step):
        cx = lax.rem(x + step, RING) if axis == "x" else x
        cy = lax.rem(y + step, RING) if axis == "y" else y
        cz = lax.rem(z + step, RING) if axis == "z" else z
        return place(cx, cy, cz)

    def pick(condition, a, b):
        return tuple(jnp.where(condition, p, q) for p, q in zip(a, b))

    zero = core == 0
    slab = jnp.where(zero, y, z)
    low = slab < CUT
    side = jnp.where(zero, z, y)

    mate = (inner + 1 - 2 * core, outer)

    parts = 8
    size = grads.shape[-1] // parts
    loads = [
        pltpu.make_async_copy(
            grads.at[:, :, pl.ds(i * size, size)], raw.at[:, :, pl.ds(i * size, size)], load_sem.at[i]
        )
        for i in range(parts)
    ]
    for load in loads:
        load.start()
    state_loads = [
        pltpu.make_async_copy(ref, state.at[i], state_sem.at[i])
        for i, ref in enumerate((master, moment, second))
    ]
    for load in state_loads:
        load.start()

    barrier = pltpu.get_barrier_semaphore()

    @pl.when(zero)
    def _():
        pl.semaphore_signal(barrier, inc=1, device_id=mate, device_id_type=MESH)

    count = 0
    for step in ORDER:
        for axis in ("x", "y", "z"):
            to_inner, to_outer = along(axis, step)
            pl.semaphore_signal(barrier, inc=1, device_id=(to_inner - core, to_outer), device_id_type=MESH)
            count += 2

    @pl.when(core == 1)
    def _():
        pl.semaphore_wait(barrier, 1)
        pl.semaphore_signal(entered, inc=1, device_id=mate, device_id_type=MESH)

    block = SHARE * 16

    def piece(at_hi, at_z, at_core):
        base = pl.multiple_of(((at_hi * 8 + at_z) * 2 + at_core) * block, block)
        return raw[0, :, pl.ds(base, block)].astype(jnp.float32).reshape(2, 8, 8, 128)

    def tile(a, b):
        return jnp.concatenate([a, b], axis=-2).astype(jnp.bfloat16)

    for part in range(parts):
        loads[part].wait()
        at_hi = part // 2
        for at_z in range(part % 2 * 4, part % 2 * 4 + 4, 2):
            even, odd = piece(at_hi, at_z, 0), piece(at_hi, at_z + 1, 0)
            half_a[0, at_z, :, at_hi] = tile(even[0, :CUT], even[1, :CUT])
            half_a[0, at_z + 1, :, at_hi] = tile(odd[0, :CUT], odd[1, :CUT])
            for lo in range(2):
                half_b[0, at_hi * 2 + lo, :, at_z // 2] = tile(even[lo, CUT:], odd[lo, CUT:])
            for slab_z in (at_z, at_z + 1):
                values = piece(at_hi, slab_z, 1)
                if slab_z < CUT:
                    half_a[1, :, slab_z, at_hi] = tile(values[0], values[1])
                else:
                    for lo in range(2):
                        half_b[1, at_hi * 2 + lo, slab_z - CUT] = values[lo].reshape(4, 16, 128).astype(jnp.bfloat16)

    @pl.when(zero)
    def _():
        pl.semaphore_wait(entered, 1)

    def send(src, dst, send_sem, recv_sem, to):
        copy = pltpu.make_async_remote_copy(
            src_ref=src, dst_ref=dst, send_sem=send_sem, recv_sem=recv_sem, device_id=to, device_id_type=MESH
        )
        copy.start()
        return copy

    def landed(ref, sem):
        pltpu.make_async_copy(ref, ref, sem).wait()

    def swap(order):
        for p, n in order:
            half, arrived = ((half_a, core_a), (half_b, core_b))[p]
            send(half.at[1 - core, n], arrived.at[n], core_send.at[p, n], core_recv.at[p, n], mate)

    @pl.when(zero)
    def _():
        swap([(0, n) for n in range(RING)] + [(1, n) for n in range(RING)])

    @pl.when(core == 1)
    def _():
        early = [(0, n) for n in range(EARLY)] + [(1, n) for n in range(RING)]
        swap(early + [(0, n) for n in range(EARLY, RING)])

    @pl.when(zero)
    def _():
        pl.semaphore_wait(barrier, count)
        pl.semaphore_signal(entered, inc=1, device_id=mate, device_id_type=MESH)

    @pl.when(core == 1)
    def _():
        pl.semaphore_wait(entered, 1)

    for step in ORDER:
        for axis in ("x", "z"):
            pl.semaphore_signal(known, inc=1, device_id=along(axis, step), device_id_type=MESH)

    steps = ORDER + (0,)
    first, rest = slice(0, EARLY // 2), slice(EARLY // 2, 4)

    def total(half, arrived, c, at, t, pairs=slice(0, 4)):
        return half[c, at, t, pairs].astype(jnp.float32) + arrived[at, t, pairs].astype(jnp.float32)

    def add_send(p, c, at, step, ts, pairs, row, to):
        half, arrived, landing = ((half_a, core_a, from_a), (half_b, core_b, from_b))[p]
        for t in ts:
            half[c, at, t, pairs] = total(half, arrived, c, at, t, pairs).astype(jnp.bfloat16)
        rows, columns = pl.ds(ts[0], len(ts)), pl.ds(pairs.start, pairs.stop - pairs.start)
        send(
            half.at[c, at, rows, columns], landing.at[step, rows, columns],
            one_send.at[row, step], one_recv.at[row, step], to,
        )

    def keep(p, c, at, ts, pairs):
        half, arrived = ((half_a, core_a), (half_b, core_b))[p]
        shares = slice(2 * pairs.start, 2 * pairs.stop)
        for t in ts:
            value = total(half, arrived, c, at, t, pairs)
            part_one[p * CUT + t, shares] = value.reshape(-1, 8, 128)

    def take(p, ts, pairs, row):
        landing = (from_a, from_b)[p]
        rows, columns = pl.ds(ts[0], len(ts)), pl.ds(pairs.start, pairs.stop - pairs.start)
        shares = slice(2 * pairs.start, 2 * pairs.stop)
        for step in ORDER:
            landed(landing.at[step, rows, columns], one_recv.at[row, step])
            for t in ts:
                value = landing[step, t, pairs].astype(jnp.float32)
                part_one[p * CUT + t, shares] += value.reshape(-1, 8, 128)

    def hand(s, t, own, to):
        @pl.when(jnp.logical_or(s != slab, t != own))
        def _():
            send(part_one.at[s, t], from_two.at[slab * 8 + own], two_send, two_recv, to)

    slabs_a, slabs_b, whole = tuple(range(CUT)), tuple(range(RING - CUT)), slice(0, 4)

    @pl.when(zero)
    def _():
        for n in range(EARLY):
            landed(core_a.at[n], core_recv.at[0, n])
            step = lax.rem(n - z + RING, RING)

            @pl.when(step != 0)
            def _():
                add_send(0, 0, n, step, slabs_a, whole, 0, place(x, y, n))

            @pl.when(step == 0)
            def _():
                keep(0, 0, n, slabs_a, whole)

        for step in steps:
            at = lax.rem(x + step, RING)
            landed(core_b.at[at], core_recv.at[1, at])
            if step:
                add_send(1, 0, at, step, slabs_b, first, 1, along("x", step))
            else:
                keep(1, 0, at, slabs_b, first)
        for step in steps:
            n = lax.rem(z + step, RING)

            @pl.when(n >= EARLY)
            def _():
                landed(core_a.at[n], core_recv.at[0, n])
                if step:
                    add_send(0, 0, n, step, slabs_a, whole, 0, along("z", step))
                else:
                    keep(0, 0, n, slabs_a, whole)

            at = lax.rem(x + step, RING)
            if step:
                add_send(1, 0, at, step, slabs_b, rest, 2, along("x", step))
            else:
                keep(1, 0, at, slabs_b, rest)

        def plane_a():
            take(0, slabs_a, whole, 0)
            for step in steps:
                for far in range(CUT):
                    s, t = lax.rem(slab + far, CUT), lax.rem(x + step, RING)
                    hand(s, t, x, place(t, s, z))

        def plane_b(low_z, high_z):
            for far in range(high_z - low_z):
                for step in range(RING - CUT):
                    s = CUT + lax.rem(slab + step, RING - CUT)
                    t = low_z + lax.rem(z + far, high_z - low_z)
                    hand(s, t, z, place(x, s, t))

        pl.semaphore_wait(known, 2 * len(ORDER))
        pl.when(z < EARLY)(plane_a)
        take(1, slabs_b, first, 1)
        plane_b(0, EARLY)
        pl.when(z >= EARLY)(plane_a)
        take(1, slabs_b, rest, 2)
        plane_b(EARLY, RING)

    @pl.when(core == 1)
    def _():
        for step in steps:
            at = lax.rem(y + step, RING)
            landed(core_a.at[at], core_recv.at[0, at])
            if step:
                add_send(0, 1, at, step, slabs_a[:EARLY], whole, 0, along("y", step))
            else:
                keep(0, 1, at, slabs_a[:EARLY], whole)
        for step in steps:
            at, at_x = lax.rem(y + step, RING), lax.rem(x + step, RING)
            landed(core_b.at[at_x], core_recv.at[1, at_x])
            if step:
                add_send(1, 1, at_x, step, slabs_b, whole, 1, along("x", step))
                add_send(0, 1, at, step, slabs_a[EARLY:], whole, 2, along("y", step))
            else:
                keep(1, 1, at_x, slabs_b, whole)
                keep(0, 1, at, slabs_a[EARLY:], whole)

        def plane_a(low_z, high_z):
            for step in steps:
                for far in range(high_z - low_z):
                    s = low_z + lax.rem(slab + far, high_z - low_z)
                    t = lax.rem(x + step, RING)
                    hand(s, t, x, place(t, y, s))

        pl.semaphore_wait(known, 2 * len(ORDER))
        take(0, slabs_a[:EARLY], whole, 0)
        plane_a(0, EARLY)
        take(0, slabs_a[EARLY:], whole, 2)
        plane_a(EARLY, CUT)
        take(1, slabs_b, whole, 1)
        for step in steps:
            for far in range(RING - CUT):
                s = CUT + lax.rem(slab + far, RING - CUT)
                t = lax.rem(y + step, RING)
                hand(s, t, y, place(x, t, s))

    third = jnp.where(low, x, side)
    from_two[slab * 8 + third] = part_one[slab, third]
    for load in state_loads:
        load.wait()
    arrived = from_two.at[pl.ds(0, RING * RING - 1)]
    pltpu.make_async_copy(arrived, arrived, two_recv).wait()
    gradient = jnp.sum(from_two[...], axis=0)

    new_master, new_moment, new_second = adamw(gradient, state[0], state[1], state[2])
    result[outer] = new_master

    all_copies = []
    for step in ORDER + (0,):
        for flip in (1, 0):
            if step or flip:
                k = len(all_copies)
                other = (x_lo + flip - 2 * flip * x_lo) * 8 + lax.rem(y + step, RING)
                all_copies.append(send(
                    result.at[outer], result.at[outer], all_send.at[k], all_recv.at[k], (inner, other)
                ))
    result[16] = new_master
    result[17] = new_moment
    result[18] = new_second
    for n in range(RING):
        landed(core_a.at[n], core_send.at[0, n])
        landed(core_b.at[n], core_send.at[1, n])

    @pl.when(zero)
    def _():
        for step in ORDER:
            landed(from_a.at[step], one_send.at[0, step])
            landed(from_b.at[step, :, pl.ds(0, EARLY // 2)], one_send.at[1, step])
            landed(from_b.at[step, :, pl.ds(EARLY // 2, 4 - EARLY // 2)], one_send.at[2, step])

    @pl.when(core == 1)
    def _():
        for step in ORDER:
            landed(from_a.at[step, pl.ds(0, EARLY)], one_send.at[0, step])
            landed(from_b.at[step], one_send.at[1, step])
            landed(from_a.at[step, pl.ds(EARLY, CUT - EARLY)], one_send.at[2, step])

    pltpu.make_async_copy(arrived, arrived, two_send).wait()
    for copy in all_copies[::-1]:
        copy.wait_recv()
    for copy in all_copies:
        copy.wait_send()


def finish(result, params_out, master_out, moment_out, second_out):
    params_out[...] = result[:16].reshape(128, 128).astype(jnp.bfloat16)
    master_out[...] = result[16]
    moment_out[...] = result[17]
    second_out[...] = result[18]


def per_device(grads, master, moment, second):
    shares = [a.reshape(8, 128) for a in (master, moment, second)]
    bf16, f32 = jnp.bfloat16, jnp.float32
    vmem = pl.BlockSpec(memory_space=pltpu.VMEM)
    hbm = pl.BlockSpec(memory_space=pl.ANY)
    dma = pltpu.SemaphoreType.DMA
    rest = RING - CUT
    result = pl.pallas_call(
        kernel,
        out_shape=jax.ShapeDtypeStruct((19, 8, 128), f32),
        in_specs=[hbm] * 4,
        out_specs=vmem,
        scratch_shapes=[
            pltpu.VMEM(grads.shape, bf16),
            pltpu.VMEM((2, 8, CUT, 4, 16, 128), bf16),
            pltpu.VMEM((2, 8, rest, 4, 16, 128), bf16),
            pltpu.VMEM((8, CUT, 4, 16, 128), bf16),
            pltpu.VMEM((8, rest, 4, 16, 128), bf16),
            pltpu.VMEM((8, CUT, 4, 16, 128), bf16),
            pltpu.VMEM((8, rest, 4, 16, 128), bf16),
            pltpu.VMEM((8, 8, 8, 128), f32),
            pltpu.VMEM((64, 8, 128), f32),
            pltpu.VMEM((3, 8, 128), f32),
            dma((8,)), dma((3,)),
            dma((2, 8)), dma((2, 8)),
            dma((3, 8)), dma((3, 8)),
            dma, dma,
            dma((15,)), dma((15,)),
            pltpu.SemaphoreType.REGULAR, pltpu.SemaphoreType.REGULAR,
        ],
        compiler_params=pltpu.CompilerParams(
            collective_id=0, has_side_effects=True, vmem_limit_bytes=VMEM_LIMIT
        ),
    )(*(pltpu.with_memory_space_constraint(a, pltpu.HBM) for a in (grads, *shares)))
    params, *outs = pl.pallas_call(
        finish,
        out_shape=[jax.ShapeDtypeStruct((128, 128), bf16)] + [jax.ShapeDtypeStruct((8, 128), f32)] * 3,
        in_specs=[vmem],
        out_specs=[vmem] * 4,
        compiler_params=pltpu.CompilerParams(vmem_limit_bytes=VMEM_LIMIT),
    )(result)
    return (params.reshape(-1), *(a.reshape(-1) for a in outs))


def solution(mesh):
    in_specs = (
        P("outer", "inner", None),
        P(("inner", "outer")),
        P(("inner", "outer")),
        P(("inner", "outer")),
    )
    out_specs = (P("inner"), P(("inner", "outer")), P(("inner", "outer")), P(("inner", "outer")))
    return jax.shard_map(
        per_device, mesh=mesh, in_specs=in_specs, out_specs=out_specs, check_vma=False
    )
```
